32 devices in a mesh: user: 4 (over y, core), party: 8 (over z, x).
Axes of the slice: x: 2, y: 2, z: 4, core: 2. Of those that a mesh axis runs over, the one named last changes fastest.
Arguments:
- ratings: bfloat16 [512, 4096], P('party', 'user'), may hold values from -6 to 6
- rating_mask: int32 [512, 4096], P('party', 'user'), may hold values 0 or 1
- user_factors: bfloat16 [4096, 256], P('user'), may hold values from -0.375 to 0.375
- item_factors: bfloat16 [512, 256], replicated, may hold values from -6 to 6
- item_index: int32 [512], replicated, may hold values from 0 to 511, each once
- features: bfloat16 [512, 524288], P(None, ('user', 'party')), may hold values from -6 to 6
- ridge_weights: bfloat16 [524288, 256], P(('user', 'party')), may hold values from -10 to 10
Outputs:
- new_factors: float32 [512, 256], P('party')
- fitted_weights: float32 [524288, 256], P(('user', 'party'))
The draws below stay inside these ranges and needn't reach their ends.
Inputs may be any that keep to these rules, and one draw needn't show every extreme that they name: `item_index`: each window item stands at exactly one tile position.
All inputs are finite; a program needn't handle non-finite values. No bound on the sum of `rating_mask` on one device may be relied on, other than what follows from the above.
Results may differ from the reference program's by a relative error of at most 0.00032.
Values may be sent and summed in bfloat16 or wider, within the bound.
A program may use at most 128 MiB of HBM per device.

```python
import jax
import jax.numpy as jnp
from jax import lax

R = 256
F = 524288
ITERS = 2
ITEMS = 512
USERS = 4096


def draw_ridge_weights(key, part):
    base_key, row_key, col_key = jax.random.split(jax.random.fold_in(key, 11), 3)
    position = jnp.arange(F, dtype=jnp.float32).reshape(F, 1) / float(F)
    base = jnp.clip(jax.random.normal(base_key, (F, R), jnp.float32), -3.5, 3.5)
    ramp = 1.15 * position
    row_scale = jnp.exp(ramp + jax.random.uniform(row_key, (F, 1), jnp.float32, -0.6, 0.6))
    col_scale = jnp.exp(jax.random.uniform(col_key, (1, R), jnp.float32, -0.6, 0.6))
    return (0.25 * base * row_scale * col_scale).astype(jnp.bfloat16)


def with_ends(entries, stream_key, low, high):
    spot = [jax.random.randint(jax.random.fold_in(stream_key, axis), (), 0, length) for axis, length in enumerate(entries.shape)]
    main_axis = entries.shape.index(max(entries.shape))
    beside = spot[:main_axis] + [(spot[main_axis] + 1) % entries.shape[main_axis]] + spot[main_axis + 1:]
    return entries.at[tuple(spot)].set(low).at[tuple(beside)].set(high)


def shard_levels(key, extent, shards, smallest, high):
    level = 1.0
    for axis_at, parts in shards:
        draws = jax.random.uniform(jax.random.fold_in(jax.random.fold_in(key, 6), axis_at), (parts,), jnp.float32, smallest / len(shards), high / len(shards))
        level = level * jnp.repeat(jnp.exp(draws), extent[axis_at] // parts).reshape((-1,) + (1,) * (len(extent) - 1 - axis_at))
    return level


def normal_values(stream_key, dims, spread, reach, cuts=(), kind=jnp.bfloat16):
    drawn = jax.random.normal(stream_key, dims, jnp.float32) * spread
    if len(cuts) > 0:
        drawn = shard_levels(stream_key, dims, cuts, -0.22, 0.18) * drawn
    return jnp.clip(drawn, min=-reach, max=reach).astype(kind)


def setup_inputs(seed: int = 0) -> dict:
    seeds = jax.random.split(jax.random.key(seed), 8)
    return {
        "ratings": normal_values(seeds[0], (ITEMS, USERS), 1.0, 6.0, ((0, 8), (1, 4))),
        "rating_mask": with_ends((jax.random.randint(seeds[1], (ITEMS, USERS), 0, 2) < 1).astype(jnp.int32), jax.random.fold_in(seeds[1], 1), 0, 1),
        "user_factors": normal_values(seeds[2], (USERS, R), R ** -0.5, 0.375, ((0, 4),)),
        "item_factors": normal_values(seeds[3], (ITEMS, R), 1.0, 6.0),
        "item_index": jax.random.permutation(seeds[4], ITEMS).astype(jnp.int32),
        "features": normal_values(seeds[5], (ITEMS, F), 1.0, 6.0, ((1, 32),)),
        "ridge_weights": draw_ridge_weights(jax.random.fold_in(seeds[7], 71), 0),
    }


learn_rate = 0.05
factor_decay = 1.0
ridge_decay = 0.05
ridge_step = 0.05

def reference(ratings, rating_mask, user_factors, item_factors, item_index, features, ridge_weights):
    tile_rows = item_factors[item_index.astype(jnp.int32)]
    scores = lax.dot_general(tile_rows, user_factors, (((1,), (1,)), ((), ())), preferred_element_type=jnp.float32)
    misfit = (rating_mask.astype(jnp.float32) * (scores - ratings.astype(jnp.float32))).astype(jnp.bfloat16)
    item_grad = jnp.dot(misfit, user_factors, preferred_element_type=jnp.float32)
    tile_wide = tile_rows.astype(jnp.float32)
    new_factors = tile_wide - learn_rate * (item_grad + factor_decay * tile_wide)
    targets = jnp.zeros((ITEMS, R), jnp.float32).at[item_index.astype(jnp.int32)].set(new_factors)
    feature_scale = 1.0 / math_sqrt(F)
    weights = ridge_weights.astype(jnp.float32)
    for iteration in range(ITERS):
        weights_bf = weights.astype(jnp.bfloat16)
        prediction = jnp.dot(features, weights_bf, preferred_element_type=jnp.float32) * feature_scale
        error_rows = (prediction - targets).astype(jnp.bfloat16)
        grad = lax.dot_general(features, error_rows, (((0,), (0,)), ((), ())), preferred_element_type=jnp.float32) * feature_scale + ridge_decay * weights
        mean_sq = jnp.mean(grad * grad)
        weights = weights - ridge_step * grad / jnp.sqrt(mean_sq + 1e-06)
    return (new_factors, weights)

def math_sqrt(value):
    return float(value) ** 0.5
```

```python
import functools

import jax
import jax.numpy as jnp
from jax import lax
from jax.experimental import pallas as pl
from jax.experimental.pallas import tpu as pltpu
from jax.sharding import PartitionSpec as P

learn_rate = 0.05
factor_decay = 1.0
ridge_decay = 0.05
ridge_step = 0.05

MESH = pl.DeviceIdType.MESH
TILE = 256


def dot32(a, b, dims):
    return lax.dot_general(a, b, (dims, ((), ())), preferred_element_type=jnp.float32)


def blocks_of(items):
    count = items // TILE
    return [(i, j) for i in range(count) for j in range(i + 1)]


def rows_of(items, devices):
    used = 2 * items + TILE * len(blocks_of(items))
    step = 8 * devices
    return -(-used // step) * step


def moments_kernel(items, used, share_ref, features_ref, weights_ref, out_ref, norm_ref):
    step = pl.program_id(0)
    gram = 2 * items

    @pl.when(step == 0)
    def _():
        out_ref[...] = jnp.zeros_like(out_ref)
        out_ref[items : 2 * items] = share_ref[...]
        norm_ref[...] = jnp.zeros_like(norm_ref)

    w = weights_ref[...]
    out_ref[0:items] += dot32(features_ref[...], w, ((1,), (0,)))
    for at, (i, j) in enumerate(blocks_of(items)):
        low = gram + at * TILE
        out_ref[low : low + TILE] += dot32(
            features_ref[i * TILE : (i + 1) * TILE],
            features_ref[j * TILE : (j + 1) * TILE],
            ((1,), (1,)),
        )
    wide = w.astype(jnp.float32)
    columns = jnp.sum(wide * wide, axis=0, keepdims=True)
    half = TILE // 2
    norm_ref[...] += columns[:, :half] + columns[:, half:]

    @pl.when(step == pl.num_programs(0) - 1)
    def _():
        out_ref[gram : gram + 1, half:] = norm_ref[...]


def moments(share, features, weights, total_rows):
    items, depth = features.shape
    rank = weights.shape[1]
    block = min(2048, depth)
    return pl.pallas_call(
        functools.partial(moments_kernel, items, total_rows),
        grid=(depth // block,),
        out_shape=jax.ShapeDtypeStruct((total_rows, rank), jnp.float32),
        in_specs=[
            pl.BlockSpec((items, rank), lambda i: (0, 0)),
            pl.BlockSpec((items, block), lambda i: (0, i)),
            pl.BlockSpec((block, rank), lambda i: (i, 0)),
        ],
        out_specs=pl.BlockSpec((total_rows, rank), lambda i: (0, 0)),
        scratch_shapes=[pltpu.VMEM((1, TILE // 2), jnp.float32)],
        compiler_params=pltpu.CompilerParams(vmem_limit_bytes=48 * 2**20),
    )(share, features, weights)


def fit_kernel(
    users, parties, scale, count, part_ref, factors_ref, targets_ref, step_ref, keep_ref,
    work, all_ref, got_a, got_b, got_c, send, recv, back_send, back_recv,
):
    items, rank = factors_ref.shape
    total = work.shape[0]
    size_b, size_c = users, parties // 2
    rows_a = total // 2
    rows_b = rows_a // size_b
    rows_c = rows_b // size_c
    u, p = lax.axis_index("user"), lax.axis_index("party")
    core, at_b, at_c = lax.rem(u, 2), lax.div(u, 2) * 2 + lax.rem(p, 2), lax.div(p, 2)

    def in_b(k):
        to = lax.rem(at_b + k, size_b)
        return to, (lax.div(to, 2) * 2 + core, at_c * 2 + lax.rem(to, 2))

    def in_c(k):
        to = lax.rem(at_c + k, size_c)
        return to, (u, to * 2 + lax.rem(p, 2))

    peer_a = (lax.div(u, 2) * 2 + (1 - core), p)
    low_a = core * rows_a
    low_b = low_a + at_b * rows_b
    low_c = low_b + at_c * rows_c

    def span(low, size):
        return pl.ds(pl.multiple_of(low, 8), size)

    barrier = pltpu.get_barrier_semaphore()
    peers = [peer_a] + [in_b(k)[1] for k in range(1, size_b)] + [in_c(k)[1] for k in range(1, size_c)]
    for peer in peers:
        pl.semaphore_signal(barrier, inc=1, device_id=peer, device_id_type=MESH)
    pl.semaphore_wait(barrier, len(peers))

    def copy(src, dst, sems, at, peer):
        made = pltpu.make_async_remote_copy(
            src_ref=src, dst_ref=dst, send_sem=sems[0].at[at], recv_sem=sems[1].at[at],
            device_id=peer, device_id_type=MESH,
        )
        made.start()
        return made

    out_sems, back_sems = (send, recv), (back_send, back_recv)
    first_a, first_b, first_c = 0, 1, size_b

    first = copy(part_ref.at[span((1 - core) * rows_a, rows_a)], got_a, out_sems, first_a, peer_a)
    first.wait()
    work[span(low_a, rows_a)] = part_ref[span(low_a, rows_a)] + got_a[...]
    second = []
    for k in range(1, size_b):
        to, peer = in_b(k)
        second.append(copy(work.at[span(low_a + to * rows_b, rows_b)], got_b.at[k - 1], out_sems, first_b + k - 1, peer))
    for made in second:
        made.wait()
    value = work[span(low_b, rows_b)]
    for k in range(1, size_b):
        value = value + got_b[k - 1]
    work[span(low_b, rows_b)] = value
    third = []
    for k in range(1, size_c):
        to, peer = in_c(k)
        third.append(copy(work.at[span(low_b + to * rows_c, rows_c)], got_c.at[k - 1], out_sems, first_c + k - 1, peer))
    for made in third:
        made.wait()
    value = work[span(low_c, rows_c)]
    for k in range(1, size_c):
        value = value + got_c[k - 1]
    all_ref[span(low_c, rows_c)] = value

    for low, size, group, start in (
        (low_c, rows_c, [in_c(k)[1] for k in range(1, size_c)], first_c),
        (low_b, rows_b, [in_b(k)[1] for k in range(1, size_b)], first_b),
        (low_a, rows_a, [peer_a], first_a),
    ):
        made = [
            copy(all_ref.at[span(low, size)], all_ref.at[span(low, size)], back_sems, start + k, peer)
            for k, peer in enumerate(group)
        ]
        for one in made:
            one.wait()

    half = TILE // 2
    gram = 2 * items
    norm = jnp.sum(all_ref[gram : gram + 1, half:])
    row = lax.broadcasted_iota(jnp.int32, (TILE, TILE), 0)
    column = lax.broadcasted_iota(jnp.int32, (TILE, TILE), 1)
    corner = all_ref[gram : gram + TILE]
    all_ref[gram : gram + TILE] = jnp.where((row == 0) & (column >= half), corner.T, corner)

    def times_gram(x):
        tiles = items // TILE
        sums = [None] * tiles

        def add(i, term):
            sums[i] = term if sums[i] is None else sums[i] + term

        for at, (i, j) in enumerate(blocks_of(items)):
            block = all_ref[gram + at * TILE : gram + (at + 1) * TILE] * (scale * scale)
            high = block.astype(jnp.bfloat16)
            low = (block - high.astype(jnp.float32)).astype(jnp.bfloat16)
            for piece in (high, low):
                add(i, dot32(piece, x[j * TILE : (j + 1) * TILE], ((1,), (0,))))
                if i != j:
                    add(j, dot32(piece, x[i * TILE : (i + 1) * TILE], ((0,), (0,))))
        return jnp.concatenate(sums, axis=0)

    old = factors_ref[...].astype(jnp.float32)
    targets = old - learn_rate * (all_ref[items : 2 * items] + factor_decay * old)
    targets_ref[...] = targets
    prediction = all_ref[0:items] * scale

    def step_of(square):
        return ridge_step * lax.rsqrt(jnp.maximum(square, 0.0) / count + 1e-06)

    def total_of(x):
        return jnp.sum(jnp.sum(x, axis=0, keepdims=True), axis=1, keepdims=True)

    error1 = (prediction - targets).astype(jnp.bfloat16)
    wide1 = error1.astype(jnp.float32)
    spread1 = times_gram(error1)
    square1 = total_of(wide1 * (spread1 + 2.0 * ridge_decay * prediction)) + ridge_decay**2 * norm
    rate1 = step_of(square1)
    keep1 = 1.0 - ridge_decay * rate1
    second_prediction = keep1 * prediction - rate1 * spread1
    error2 = (second_prediction - targets).astype(jnp.bfloat16)
    wide2 = error2.astype(jnp.float32)
    spread2 = times_gram(error2)
    mixed = wide2 - (ridge_decay * rate1) * wide1
    mixed_spread = spread2 - (ridge_decay * rate1) * spread1
    square2 = (
        total_of(mixed * (mixed_spread + (2.0 * ridge_decay * keep1) * prediction))
        + (ridge_decay * keep1) * (ridge_decay * keep1) * norm
    )
    rate2 = step_of(square2)
    keep2 = 1.0 - ridge_decay * rate2
    step_ref[...] = (scale * (keep2 * rate1 * wide1 + rate2 * wide2)).astype(jnp.bfloat16)
    keep_ref[...] = jnp.broadcast_to(keep1 * keep2, keep_ref.shape)


def fit(part, factors, users, parties, scale, count):
    total, rank = part.shape
    items = factors.shape[0]
    size_b, size_c = users, parties // 2
    rows_a = total // 2
    rows_b = rows_a // size_b
    rows_c = rows_b // size_c
    copies = 1 + (size_b - 1) + (size_c - 1)
    vmem = pl.BlockSpec(memory_space=pltpu.VMEM)
    return pl.pallas_call(
        functools.partial(fit_kernel, users, parties, scale, count),
        out_shape=(
            jax.ShapeDtypeStruct((items, rank), jnp.float32),
            jax.ShapeDtypeStruct((items, rank), jnp.bfloat16),
            jax.ShapeDtypeStruct((8, 128), jnp.float32),
        ),
        in_specs=[vmem] * 2,
        out_specs=(vmem,) * 3,
        scratch_shapes=[
            pltpu.VMEM((total, rank), jnp.float32),
            pltpu.VMEM((total, rank), jnp.float32),
            pltpu.VMEM((rows_a, rank), jnp.float32),
            pltpu.VMEM((size_b - 1, rows_b, rank), jnp.float32),
            pltpu.VMEM((max(size_c - 1, 1), rows_c, rank), jnp.float32),
        ]
        + [pltpu.SemaphoreType.DMA((copies,))] * 4,
        compiler_params=pltpu.CompilerParams(
            collective_id=0, has_side_effects=True, vmem_limit_bytes=56 * 2**20
        ),
    )(part, factors)


def local(users, parties, ratings, rating_mask, user_factors, item_factors, item_index, features, ridge_weights):
    local_items = ratings.shape[0]
    items = item_factors.shape[0]
    party_pos = lax.axis_index("party")
    local_index = lax.dynamic_slice_in_dim(item_index, party_pos * local_items, local_items)
    at_item = local_index[:, None] == jnp.arange(items, dtype=jnp.int32)[None, :]
    tile_rows = jnp.dot(at_item.astype(jnp.bfloat16), item_factors)
    scores = dot32(tile_rows, user_factors, ((1,), (1,)))
    misfit = (rating_mask.astype(jnp.float32) * (scores - ratings.astype(jnp.float32))).astype(jnp.bfloat16)
    partial_grad = jnp.dot(misfit, user_factors, preferred_element_type=jnp.float32)
    share = lax.dot_general(
        at_item.astype(jnp.float32), partial_grad, (((0,), (0,)), ((), ())), precision=lax.Precision.HIGHEST
    )
    devices_all = users * parties
    total_features = features.shape[1] * devices_all
    scale = 1.0 / float(total_features) ** 0.5
    part = moments(share, features, ridge_weights, rows_of(items, devices_all))
    count = float(total_features * ridge_weights.shape[1])
    targets, step, keep = fit(part, item_factors, users, parties, scale, count)
    new_factors = jnp.take(targets, local_index, axis=0)
    weights = ridge_weights.astype(jnp.float32) * keep[0, 0] - dot32(features, step, ((0,), (0,)))
    return (new_factors, weights)


def solution(mesh):
    in_specs = (
        P("party", "user"),
        P("party", "user"),
        P("user", None),
        P(),
        P(),
        P(None, ("user", "party")),
        P(("user", "party"), None),
    )
    out_specs = (P("party", None), P(("user", "party"), None))
    body = functools.partial(local, mesh.shape["user"], mesh.shape["party"])
    return jax.shard_map(body, mesh=mesh, in_specs=in_specs, out_specs=out_specs, check_vma=False)
```

```python
import functools

import jax
import jax.numpy as jnp
from jax import lax
from jax.experimental import pallas as pl
from jax.experimental.pallas import tpu as pltpu
from jax.sharding import PartitionSpec as P

learn_rate = 0.05
factor_decay = 1.0
ridge_decay = 0.05
ridge_step = 0.05

MESH = pl.DeviceIdType.MESH
TILE = 256


def dot32(a, b, dims):
    return lax.dot_general(a, b, (dims, ((), ())), preferred_element_type=jnp.float32)


def blocks_of(items):
    count = items // TILE
    return [(i, j) for i in range(count) for j in range(i + 1)]


def rows_of(items, devices):
    used = 2 * items + TILE * len(blocks_of(items))
    step = 8 * devices
    return -(-used // step) * step


def chunks_of(total, devices):
    unit = 8 * devices
    units = total // unit
    count = min(3, units)
    return [unit * (units // count + (1 if i < units % count else 0)) for i in range(count)]


def moments_kernel(items, used, share_ref, features_ref, weights_ref, out_ref, norm_ref):
    step = pl.program_id(0)
    gram = 2 * items

    @pl.when(step == 0)
    def _():
        out_ref[...] = jnp.zeros_like(out_ref)
        out_ref[items : 2 * items] = share_ref[...]
        norm_ref[...] = jnp.zeros_like(norm_ref)

    w = weights_ref[...]
    out_ref[0:items] += dot32(features_ref[...], w, ((1,), (0,)))
    for at, (i, j) in enumerate(blocks_of(items)):
        low = gram + at * TILE
        out_ref[low : low + TILE] += dot32(
            features_ref[i * TILE : (i + 1) * TILE],
            features_ref[j * TILE : (j + 1) * TILE],
            ((1,), (1,)),
        )
    wide = w.astype(jnp.float32)
    columns = jnp.sum(wide * wide, axis=0, keepdims=True)
    half = TILE // 2
    norm_ref[...] += columns[:, :half] + columns[:, half:]

    @pl.when(step == pl.num_programs(0) - 1)
    def _():
        out_ref[gram : gram + 1, half:] = norm_ref[...]


def moments(share, features, weights, total_rows):
    items, depth = features.shape
    rank = weights.shape[1]
    block = min(2048, depth)
    return pl.pallas_call(
        functools.partial(moments_kernel, items, total_rows),
        grid=(depth // block,),
        out_shape=jax.ShapeDtypeStruct((total_rows, rank), jnp.float32),
        in_specs=[
            pl.BlockSpec((items, rank), lambda i: (0, 0)),
            pl.BlockSpec((items, block), lambda i: (0, i)),
            pl.BlockSpec((block, rank), lambda i: (i, 0)),
        ],
        out_specs=pl.BlockSpec((total_rows, rank), lambda i: (0, 0)),
        scratch_shapes=[pltpu.VMEM((1, TILE // 2), jnp.float32)],
        compiler_params=pltpu.CompilerParams(vmem_limit_bytes=48 * 2**20),
    )(share, features, weights)


def fit_kernel(
    users, parties, scale, count, part_ref, factors_ref, targets_ref, step_ref, keep_ref,
    work, all_ref, got_a, got_b, got_c, send, recv, back_send, back_recv,
):
    items, rank = factors_ref.shape
    total = work.shape[0]
    size_b, size_c = users, parties // 2
    u, p = lax.axis_index("user"), lax.axis_index("party")
    core, at_b, at_c = lax.rem(u, 2), lax.div(u, 2) * 2 + lax.rem(p, 2), lax.div(p, 2)

    def in_b(k):
        to = lax.rem(at_b + k, size_b)
        return to, (lax.div(to, 2) * 2 + core, at_c * 2 + lax.rem(to, 2))

    def in_c(k):
        to = lax.rem(at_c + k, size_c)
        return to, (u, to * 2 + lax.rem(p, 2))

    peer_a = (lax.div(u, 2) * 2 + (1 - core), p)

    def span(low, size):
        return pl.ds(pl.multiple_of(low, 8), size)

    barrier = pltpu.get_barrier_semaphore()
    peers = [peer_a] + [in_b(k)[1] for k in range(1, size_b)] + [in_c(k)[1] for k in range(1, size_c)]
    for peer in peers:
        pl.semaphore_signal(barrier, inc=1, device_id=peer, device_id_type=MESH)
    pl.semaphore_wait(barrier, len(peers))

    def copy(src, dst, sems, at, peer):
        made = pltpu.make_async_remote_copy(
            src_ref=src, dst_ref=dst, send_sem=sems[0].at[at], recv_sem=sems[1].at[at],
            device_id=peer, device_id_type=MESH,
        )
        made.start()
        return made

    out_sems, back_sems = (send, recv), (back_send, back_recv)
    first_a, first_b, first_c = 0, 1, size_b

    per_chunk = 1 + (size_b - 1) + (size_c - 1)
    chunks = []
    base = 0
    for at, rows in enumerate(chunks_of(total, users * parties)):
        a, b, c = rows // 2, rows // 2 // size_b, rows // 2 // size_b // size_c
        chunks.append((base, a, b, c, base // 2, base // 2 // size_b, base // 2 // size_b // size_c, at * per_chunk))
        base += rows

    def lows(base, a, b, c):
        low_a = base + core * a
        low_b = low_a + at_b * b
        return low_a, low_b, low_b + at_c * c

    first, second, third = [], [], []
    for base, a, b, c, in_a, _, _, sem in chunks:
        first.append(copy(part_ref.at[span(base + (1 - core) * a, a)], got_a.at[pl.ds(in_a, a)], out_sems, sem + first_a, peer_a))
    for at, (base, a, b, c, in_a, slot_b, _, sem) in enumerate(chunks):
        low_a, low_b, low_c = lows(base, a, b, c)
        first[at].wait()
        work[span(low_a, a)] = part_ref[span(low_a, a)] + got_a[in_a : in_a + a]
        made = []
        for k in range(1, size_b):
            to, peer = in_b(k)
            made.append(copy(work.at[span(low_a + to * b, b)], got_b.at[k - 1, pl.ds(slot_b, b)], out_sems, sem + first_b + k - 1, peer))
        second.append(made)
    for at, (base, a, b, c, _, slot_b, slot_c, sem) in enumerate(chunks):
        low_a, low_b, low_c = lows(base, a, b, c)
        for one in second[at]:
            one.wait()
        value = work[span(low_b, b)]
        for k in range(1, size_b):
            value = value + got_b[k - 1, slot_b : slot_b + b]
        work[span(low_b, b)] = value
        made = []
        for k in range(1, size_c):
            to, peer = in_c(k)
            made.append(copy(work.at[span(low_b + to * c, c)], got_c.at[k - 1, pl.ds(slot_c, c)], out_sems, sem + first_c + k - 1, peer))
        third.append(made)

    def back(low, size, group, start):
        return [
            copy(all_ref.at[span(low, size)], all_ref.at[span(low, size)], back_sems, start + k, peer)
            for k, peer in enumerate(group)
        ]

    peers_b = [in_b(k)[1] for k in range(1, size_b)]
    peers_c = [in_c(k)[1] for k in range(1, size_c)]
    stage_c, stage_b, stage_a = [], [], []
    for at, (base, a, b, c, _, _, slot_c, sem) in enumerate(chunks):
        low_a, low_b, low_c = lows(base, a, b, c)
        for one in third[at]:
            one.wait()
        value = work[span(low_c, c)]
        for k in range(1, size_c):
            value = value + got_c[k - 1, slot_c : slot_c + c]
        all_ref[span(low_c, c)] = value
        stage_c.append(back(low_c, c, peers_c, sem + first_c))
    for at, (base, a, b, c, _, _, _, sem) in enumerate(chunks):
        low_a, low_b, low_c = lows(base, a, b, c)
        for one in stage_c[at]:
            one.wait()
        stage_b.append(back(low_b, b, peers_b, sem + first_b))
    for at, (base, a, b, c, _, _, _, sem) in enumerate(chunks):
        low_a, low_b, low_c = lows(base, a, b, c)
        for one in stage_b[at]:
            one.wait()
        stage_a.append(back(low_a, a, [peer_a], sem + first_a))
    for made in stage_a:
        for one in made:
            one.wait()

    half = TILE // 2
    gram = 2 * items
    norm = jnp.sum(all_ref[gram : gram + 1, half:])
    row = lax.broadcasted_iota(jnp.int32, (TILE, TILE), 0)
    column = lax.broadcasted_iota(jnp.int32, (TILE, TILE), 1)
    corner = all_ref[gram : gram + TILE]
    all_ref[gram : gram + TILE] = jnp.where((row == 0) & (column >= half), corner.T, corner)

    def times_gram(x):
        tiles = items // TILE
        sums = [None] * tiles

        def add(i, term):
            sums[i] = term if sums[i] is None else sums[i] + term

        for at, (i, j) in enumerate(blocks_of(items)):
            block = all_ref[gram + at * TILE : gram + (at + 1) * TILE] * (scale * scale)
            high = block.astype(jnp.bfloat16)
            low = (block - high.astype(jnp.float32)).astype(jnp.bfloat16)
            for piece in (high, low):
                add(i, dot32(piece, x[j * TILE : (j + 1) * TILE], ((1,), (0,))))
                if i != j:
                    add(j, dot32(piece, x[i * TILE : (i + 1) * TILE], ((0,), (0,))))
        return jnp.concatenate(sums, axis=0)

    old = factors_ref[...].astype(jnp.float32)
    targets = old - learn_rate * (all_ref[items : 2 * items] + factor_decay * old)
    targets_ref[...] = targets
    prediction = all_ref[0:items] * scale

    def step_of(square):
        return ridge_step * lax.rsqrt(jnp.maximum(square, 0.0) / count + 1e-06)

    def total_of(x):
        return jnp.sum(jnp.sum(x, axis=0, keepdims=True), axis=1, keepdims=True)

    error1 = (prediction - targets).astype(jnp.bfloat16)
    wide1 = error1.astype(jnp.float32)
    spread1 = times_gram(error1)
    square1 = total_of(wide1 * (spread1 + 2.0 * ridge_decay * prediction)) + ridge_decay**2 * norm
    rate1 = step_of(square1)
    keep1 = 1.0 - ridge_decay * rate1
    second_prediction = keep1 * prediction - rate1 * spread1
    error2 = (second_prediction - targets).astype(jnp.bfloat16)
    wide2 = error2.astype(jnp.float32)
    spread2 = times_gram(error2)
    mixed = wide2 - (ridge_decay * rate1) * wide1
    mixed_spread = spread2 - (ridge_decay * rate1) * spread1
    square2 = (
        total_of(mixed * (mixed_spread + (2.0 * ridge_decay * keep1) * prediction))
        + (ridge_decay * keep1) * (ridge_decay * keep1) * norm
    )
    rate2 = step_of(square2)
    keep2 = 1.0 - ridge_decay * rate2
    step_ref[...] = (scale * (keep2 * rate1 * wide1 + rate2 * wide2)).astype(jnp.bfloat16)
    keep_ref[...] = jnp.broadcast_to(keep1 * keep2, keep_ref.shape)


def fit(part, factors, users, parties, scale, count):
    total, rank = part.shape
    items = factors.shape[0]
    size_b, size_c = users, parties // 2
    rows_a = total // 2
    rows_b = rows_a // size_b
    rows_c = rows_b // size_c
    copies = (1 + (size_b - 1) + (size_c - 1)) * len(chunks_of(total, users * parties))
    vmem = pl.BlockSpec(memory_space=pltpu.VMEM)
    return pl.pallas_call(
        functools.partial(fit_kernel, users, parties, scale, count),
        out_shape=(
            jax.ShapeDtypeStruct((items, rank), jnp.float32),
            jax.ShapeDtypeStruct((items, rank), jnp.bfloat16),
            jax.ShapeDtypeStruct((8, 128), jnp.float32),
        ),
        in_specs=[vmem] * 2,
        out_specs=(vmem,) * 3,
        scratch_shapes=[
            pltpu.VMEM((total, rank), jnp.float32),
            pltpu.VMEM((total, rank), jnp.float32),
            pltpu.VMEM((rows_a, rank), jnp.float32),
            pltpu.VMEM((size_b - 1, rows_b, rank), jnp.float32),
            pltpu.VMEM((max(size_c - 1, 1), rows_c, rank), jnp.float32),
        ]
        + [pltpu.SemaphoreType.DMA((copies,))] * 4,
        compiler_params=pltpu.CompilerParams(
            collective_id=0, has_side_effects=True, vmem_limit_bytes=56 * 2**20
        ),
    )(part, factors)


def last_kernel(features_ref, weights_ref, step_ref, keep_ref, out_ref):
    change = dot32(features_ref[...], step_ref[...], ((0,), (0,)))
    out_ref[...] = weights_ref[...].astype(jnp.float32) * keep_ref[0:1, 0:1] - change


def last(features, weights, step, keep):
    items, depth = features.shape
    rank = weights.shape[1]
    block = min(1024, depth)
    return pl.pallas_call(
        last_kernel,
        grid=(depth // block,),
        out_shape=jax.ShapeDtypeStruct((depth, rank), jnp.float32),
        in_specs=[
            pl.BlockSpec((items, block), lambda i: (0, i)),
            pl.BlockSpec((block, rank), lambda i: (i, 0)),
            pl.BlockSpec((items, rank), lambda i: (0, 0)),
            pl.BlockSpec(keep.shape, lambda i: (0, 0)),
        ],
        out_specs=pl.BlockSpec((block, rank), lambda i: (i, 0)),
        compiler_params=pltpu.CompilerParams(vmem_limit_bytes=48 * 2**20),
    )(features, weights, step, keep)


def local(users, parties, ratings, rating_mask, user_factors, item_factors, item_index, features, ridge_weights):
    local_items = ratings.shape[0]
    items = item_factors.shape[0]
    party_pos = lax.axis_index("party")
    local_index = lax.dynamic_slice_in_dim(item_index, party_pos * local_items, local_items)
    at_item = local_index[:, None] == jnp.arange(items, dtype=jnp.int32)[None, :]
    tile_rows = jnp.dot(at_item.astype(jnp.bfloat16), item_factors)
    scores = dot32(tile_rows, user_factors, ((1,), (1,)))
    misfit = (rating_mask.astype(jnp.float32) * (scores - ratings.astype(jnp.float32))).astype(jnp.bfloat16)
    partial_grad = jnp.dot(misfit, user_factors, preferred_element_type=jnp.float32)
    share = lax.dot_general(
        at_item.astype(jnp.float32), partial_grad, (((0,), (0,)), ((), ())), precision=lax.Precision.HIGHEST
    )
    devices_all = users * parties
    total_features = features.shape[1] * devices_all
    scale = 1.0 / float(total_features) ** 0.5
    part = moments(share, features, ridge_weights, rows_of(items, devices_all))
    count = float(total_features * ridge_weights.shape[1])
    targets, step, keep = fit(part, item_factors, users, parties, scale, count)
    new_factors = jnp.take(targets, local_index, axis=0)
    weights = last(features, ridge_weights, step, keep)
    return (new_factors, weights)


def solution(mesh):
    in_specs = (
        P("party", "user"),
        P("party", "user"),
        P("user", None),
        P(),
        P(),
        P(None, ("user", "party")),
        P(("user", "party"), None),
    )
    out_specs = (P("party", None), P(("user", "party"), None))
    body = functools.partial(local, mesh.shape["user"], mesh.shape["party"])
    return jax.shard_map(body, mesh=mesh, in_specs=in_specs, out_specs=out_specs, check_vma=False)
```

```python
import functools

import jax
import jax.numpy as jnp
from jax import lax
from jax.experimental import pallas as pl
from jax.experimental.pallas import tpu as pltpu
from jax.sharding import PartitionSpec as P

learn_rate = 0.05
factor_decay = 1.0
ridge_decay = 0.05
ridge_step = 0.05

MESH = pl.DeviceIdType.MESH
TILE = 256


def dot32(a, b, dims):
    return lax.dot_general(a, b, (dims, ((), ())), preferred_element_type=jnp.float32)


def blocks_of(items):
    count = items // TILE
    return [(i, j) for i in range(count) for j in range(i + 1)]


def rows_of(items, devices):
    used = 2 * items + TILE * len(blocks_of(items))
    step = 8 * devices
    return -(-used // step) * step


def chunks_of(total, devices):
    unit = 8 * devices
    units = total // unit
    count = min(3, units)
    return [unit * (units // count + (1 if i < units % count else 0)) for i in range(count)]


def moments_kernel(items, used, share_ref, features_ref, weights_ref, out_ref, norm_ref):
    step = pl.program_id(0)
    gram = 2 * items

    @pl.when(step == 0)
    def _():
        out_ref[...] = jnp.zeros_like(out_ref)
        out_ref[items : 2 * items] = share_ref[...]
        norm_ref[...] = jnp.zeros_like(norm_ref)

    w = weights_ref[...]
    out_ref[0:items] += dot32(features_ref[...], w, ((1,), (0,)))
    for at, (i, j) in enumerate(blocks_of(items)):
        low = gram + at * TILE
        out_ref[low : low + TILE] += dot32(
            features_ref[i * TILE : (i + 1) * TILE],
            features_ref[j * TILE : (j + 1) * TILE],
            ((1,), (1,)),
        )
    wide = w.astype(jnp.float32)
    columns = jnp.sum(wide * wide, axis=0, keepdims=True)
    half = TILE // 2
    norm_ref[...] += columns[:, :half] + columns[:, half:]

    @pl.when(step == pl.num_programs(0) - 1)
    def _():
        out_ref[gram : gram + 1, half:] = norm_ref[...]


def moments(share, features, weights, total_rows):
    items, depth = features.shape
    rank = weights.shape[1]
    block = min(4096, depth)
    return pl.pallas_call(
        functools.partial(moments_kernel, items, total_rows),
        grid=(depth // block,),
        out_shape=jax.ShapeDtypeStruct((total_rows, rank), jnp.float32),
        in_specs=[
            pl.BlockSpec((items, rank), lambda i: (0, 0)),
            pl.BlockSpec((items, block), lambda i: (0, i)),
            pl.BlockSpec((block, rank), lambda i: (i, 0)),
        ],
        out_specs=pl.BlockSpec((total_rows, rank), lambda i: (0, 0)),
        scratch_shapes=[pltpu.VMEM((1, TILE // 2), jnp.float32)],
        compiler_params=pltpu.CompilerParams(vmem_limit_bytes=48 * 2**20),
    )(share, features, weights)


def fit_kernel(
    users, parties, scale, count, part_ref, factors_ref, targets_ref, step_ref, keep_ref,
    work, all_ref, got_a, got_b, got_c, send, recv, back_send, back_recv,
):
    items, rank = factors_ref.shape
    total = work.shape[0]
    size_b, size_c = users, parties // 2
    u, p = lax.axis_index("user"), lax.axis_index("party")
    core, at_b, at_c = lax.rem(u, 2), lax.div(u, 2) * 2 + lax.rem(p, 2), lax.div(p, 2)

    def in_b(k):
        to = lax.rem(at_b + k, size_b)
        return to, (lax.div(to, 2) * 2 + core, at_c * 2 + lax.rem(to, 2))

    def in_c(k):
        to = lax.rem(at_c + k, size_c)
        return to, (u, to * 2 + lax.rem(p, 2))

    peer_a = (lax.div(u, 2) * 2 + (1 - core), p)

    def span(low, size):
        return pl.ds(pl.multiple_of(low, 8), size)

    barrier = pltpu.get_barrier_semaphore()
    peers = [peer_a] + [in_b(k)[1] for k in range(1, size_b)] + [in_c(k)[1] for k in range(1, size_c)]
    for peer in peers:
        pl.semaphore_signal(barrier, inc=1, device_id=peer, device_id_type=MESH)
    pl.semaphore_wait(barrier, len(peers))

    def copy(src, dst, sems, at, peer):
        made = pltpu.make_async_remote_copy(
            src_ref=src, dst_ref=dst, send_sem=sems[0].at[at], recv_sem=sems[1].at[at],
            device_id=peer, device_id_type=MESH,
        )
        made.start()
        return made

    out_sems, back_sems = (send, recv), (back_send, back_recv)
    first_a, first_b, first_c = 0, 1, size_b

    per_chunk = 1 + (size_b - 1) + (size_c - 1)
    chunks = []
    base = 0
    for at, rows in enumerate(chunks_of(total, users * parties)):
        a, b, c = rows // 2, rows // 2 // size_b, rows // 2 // size_b // size_c
        chunks.append((base, a, b, c, base // 2, base // 2 // size_b, base // 2 // size_b // size_c, at * per_chunk))
        base += rows

    def lows(base, a, b, c):
        low_a = base + core * a
        low_b = low_a + at_b * b
        return low_a, low_b, low_b + at_c * c

    first, second, third = [], [], []
    for base, a, b, c, in_a, _, _, sem in chunks:
        first.append(copy(part_ref.at[span(base + (1 - core) * a, a)], got_a.at[pl.ds(in_a, a)], out_sems, sem + first_a, peer_a))
    for at, (base, a, b, c, in_a, slot_b, _, sem) in enumerate(chunks):
        low_a, low_b, low_c = lows(base, a, b, c)
        first[at].wait()
        work[span(low_a, a)] = part_ref[span(low_a, a)] + got_a[in_a : in_a + a]
        made = []
        for k in range(1, size_b):
            to, peer = in_b(k)
            made.append(copy(work.at[span(low_a + to * b, b)], got_b.at[k - 1, pl.ds(slot_b, b)], out_sems, sem + first_b + k - 1, peer))
        second.append(made)
    for at, (base, a, b, c, _, slot_b, slot_c, sem) in enumerate(chunks):
        low_a, low_b, low_c = lows(base, a, b, c)
        for one in second[at]:
            one.wait()
        value = work[span(low_b, b)]
        for k in range(1, size_b):
            value = value + got_b[k - 1, slot_b : slot_b + b]
        work[span(low_b, b)] = value
        made = []
        for k in range(1, size_c):
            to, peer = in_c(k)
            made.append(copy(work.at[span(low_b + to * c, c)], got_c.at[k - 1, pl.ds(slot_c, c)], out_sems, sem + first_c + k - 1, peer))
        third.append(made)

    def back(low, size, group, start):
        return [
            copy(all_ref.at[span(low, size)], all_ref.at[span(low, size)], back_sems, start + k, peer)
            for k, peer in enumerate(group)
        ]

    peers_b = [in_b(k)[1] for k in range(1, size_b)]
    peers_c = [in_c(k)[1] for k in range(1, size_c)]
    stage_c, stage_b, stage_a = [], [], []
    for at, (base, a, b, c, _, _, slot_c, sem) in enumerate(chunks):
        low_a, low_b, low_c = lows(base, a, b, c)
        for one in third[at]:
            one.wait()
        value = work[span(low_c, c)]
        for k in range(1, size_c):
            value = value + got_c[k - 1, slot_c : slot_c + c]
        all_ref[span(low_c, c)] = value
        stage_c.append(back(low_c, c, peers_c, sem + first_c))
    for at, (base, a, b, c, _, _, _, sem) in enumerate(chunks):
        low_a, low_b, low_c = lows(base, a, b, c)
        for one in stage_c[at]:
            one.wait()
        stage_b.append(back(low_b, b, peers_b, sem + first_b))
    for at, (base, a, b, c, _, _, _, sem) in enumerate(chunks):
        low_a, low_b, low_c = lows(base, a, b, c)
        for one in stage_b[at]:
            one.wait()
        stage_a.append(back(low_a, a, [peer_a], sem + first_a))
    for made in stage_a:
        for one in made:
            one.wait()

    half = TILE // 2
    gram = 2 * items
    norm = jnp.sum(all_ref[gram : gram + 1, half:])
    row = lax.broadcasted_iota(jnp.int32, (TILE, TILE), 0)
    column = lax.broadcasted_iota(jnp.int32, (TILE, TILE), 1)
    corner = all_ref[gram : gram + TILE]
    all_ref[gram : gram + TILE] = jnp.where((row == 0) & (column >= half), corner.T, corner)

    def times_gram(x):
        tiles = items // TILE
        sums = [None] * tiles

        def add(i, term):
            sums[i] = term if sums[i] is None else sums[i] + term

        for at, (i, j) in enumerate(blocks_of(items)):
            block = all_ref[gram + at * TILE : gram + (at + 1) * TILE] * (scale * scale)
            high = block.astype(jnp.bfloat16)
            low = (block - high.astype(jnp.float32)).astype(jnp.bfloat16)
            for piece in (high, low):
                add(i, dot32(piece, x[j * TILE : (j + 1) * TILE], ((1,), (0,))))
                if i != j:
                    add(j, dot32(piece, x[i * TILE : (i + 1) * TILE], ((0,), (0,))))
        return jnp.concatenate(sums, axis=0)

    old = factors_ref[...].astype(jnp.float32)
    targets = old - learn_rate * (all_ref[items : 2 * items] + factor_decay * old)
    targets_ref[...] = targets
    prediction = all_ref[0:items] * scale

    def step_of(square):
        return ridge_step * lax.rsqrt(jnp.maximum(square, 0.0) / count + 1e-06)

    def total_of(x):
        return jnp.sum(jnp.sum(x, axis=0, keepdims=True), axis=1, keepdims=True)

    error1 = (prediction - targets).astype(jnp.bfloat16)
    wide1 = error1.astype(jnp.float32)
    spread1 = times_gram(error1)
    square1 = total_of(wide1 * (spread1 + 2.0 * ridge_decay * prediction)) + ridge_decay**2 * norm
    rate1 = step_of(square1)
    keep1 = 1.0 - ridge_decay * rate1
    second_prediction = keep1 * prediction - rate1 * spread1
    error2 = (second_prediction - targets).astype(jnp.bfloat16)
    wide2 = error2.astype(jnp.float32)
    spread2 = times_gram(error2)
    mixed = wide2 - (ridge_decay * rate1) * wide1
    mixed_spread = spread2 - (ridge_decay * rate1) * spread1
    square2 = (
        total_of(mixed * (mixed_spread + (2.0 * ridge_decay * keep1) * prediction))
        + (ridge_decay * keep1) * (ridge_decay * keep1) * norm
    )
    rate2 = step_of(square2)
    keep2 = 1.0 - ridge_decay * rate2
    step_ref[...] = (scale * (keep2 * rate1 * wide1 + rate2 * wide2)).astype(jnp.bfloat16)
    keep_ref[...] = jnp.broadcast_to(keep1 * keep2, keep_ref.shape)


def fit(part, factors, users, parties, scale, count):
    total, rank = part.shape
    items = factors.shape[0]
    size_b, size_c = users, parties // 2
    rows_a = total // 2
    rows_b = rows_a // size_b
    rows_c = rows_b // size_c
    copies = (1 + (size_b - 1) + (size_c - 1)) * len(chunks_of(total, users * parties))
    vmem = pl.BlockSpec(memory_space=pltpu.VMEM)
    return pl.pallas_call(
        functools.partial(fit_kernel, users, parties, scale, count),
        out_shape=(
            jax.ShapeDtypeStruct((items, rank), jnp.float32),
            jax.ShapeDtypeStruct((items, rank), jnp.bfloat16),
            jax.ShapeDtypeStruct((8, 128), jnp.float32),
        ),
        in_specs=[vmem] * 2,
        out_specs=(vmem,) * 3,
        scratch_shapes=[
            pltpu.VMEM((total, rank), jnp.float32),
            pltpu.VMEM((total, rank), jnp.float32),
            pltpu.VMEM((rows_a, rank), jnp.float32),
            pltpu.VMEM((size_b - 1, rows_b, rank), jnp.float32),
            pltpu.VMEM((max(size_c - 1, 1), rows_c, rank), jnp.float32),
        ]
        + [pltpu.SemaphoreType.DMA((copies,))] * 4,
        compiler_params=pltpu.CompilerParams(
            collective_id=0, has_side_effects=True, vmem_limit_bytes=56 * 2**20
        ),
    )(part, factors)


def last_kernel(features_ref, weights_ref, step_ref, keep_ref, out_ref):
    change = dot32(features_ref[...], step_ref[...], ((0,), (0,)))
    out_ref[...] = weights_ref[...].astype(jnp.float32) * keep_ref[0:1, 0:1] - change


def last(features, weights, step, keep):
    items, depth = features.shape
    rank = weights.shape[1]
    block = min(4096, depth)
    return pl.pallas_call(
        last_kernel,
        grid=(depth // block,),
        out_shape=jax.ShapeDtypeStruct((depth, rank), jnp.float32),
        in_specs=[
            pl.BlockSpec((items, block), lambda i: (0, i)),
            pl.BlockSpec((block, rank), lambda i: (i, 0)),
            pl.BlockSpec((items, rank), lambda i: (0, 0)),
            pl.BlockSpec(keep.shape, lambda i: (0, 0)),
        ],
        out_specs=pl.BlockSpec((block, rank), lambda i: (i, 0)),
        compiler_params=pltpu.CompilerParams(vmem_limit_bytes=48 * 2**20),
    )(features, weights, step, keep)


def local(users, parties, ratings, rating_mask, user_factors, item_factors, item_index, features, ridge_weights):
    local_items = ratings.shape[0]
    items = item_factors.shape[0]
    party_pos = lax.axis_index("party")
    local_index = lax.dynamic_slice_in_dim(item_index, party_pos * local_items, local_items)
    at_item = local_index[:, None] == jnp.arange(items, dtype=jnp.int32)[None, :]
    tile_rows = jnp.dot(at_item.astype(jnp.bfloat16), item_factors)
    scores = dot32(tile_rows, user_factors, ((1,), (1,)))
    misfit = (rating_mask.astype(jnp.float32) * (scores - ratings.astype(jnp.float32))).astype(jnp.bfloat16)
    partial_grad = jnp.dot(misfit, user_factors, preferred_element_type=jnp.float32)
    share = lax.dot_general(
        at_item.astype(jnp.float32), partial_grad, (((0,), (0,)), ((), ())), precision=lax.Precision.HIGHEST
    )
    devices_all = users * parties
    total_features = features.shape[1] * devices_all
    scale = 1.0 / float(total_features) ** 0.5
    part = moments(share, features, ridge_weights, rows_of(items, devices_all))
    count = float(total_features * ridge_weights.shape[1])
    targets, step, keep = fit(part, item_factors, users, parties, scale, count)
    new_factors = jnp.take(targets, local_index, axis=0)
    weights = last(features, ridge_weights, step, keep)
    return (new_factors, weights)


def solution(mesh):
    in_specs = (
        P("party", "user"),
        P("party", "user"),
        P("user", None),
        P(),
        P(),
        P(None, ("user", "party")),
        P(("user", "party"), None),
    )
    out_specs = (P("party", None), P(("user", "party"), None))
    body = functools.partial(local, mesh.shape["user"], mesh.shape["party"])
    return jax.shard_map(body, mesh=mesh, in_specs=in_specs, out_specs=out_specs, check_vma=False)
```
